32 devices in a mesh: streams: 2 (over x), frames: 16 (over z, y, core).
Axes of the slice: x: 2, y: 2, z: 4, core: 2. Of those that a mesh axis runs over, the one named last changes fastest.
Arguments:
- features: bfloat16 [65536, 256], P(('streams', 'frames')), parts along dimension 0, may hold values from -9 to 9
- start_block: bfloat16 [65536, 128], P(('streams', 'frames')), parts along dimension 0, may hold values from -6 to 6
- counts: int32 [128], P(('streams', 'frames')), parts along dimension 0, may hold values from 128 to 512, as said below
- reach: int32 [128], P(('streams', 'frames')), parts along dimension 0, may hold values from 0 to 2, as said below
Outputs:
- basis: float32 [65536, 128], P(('streams', 'frames')), parts along dimension 0
- rayleigh: float32 [256, 128], P('streams'), parts along dimension 0
The draws below stay inside these ranges and needn't reach their ends.
There are 2 independent parts, one for each index of `streams`. The reference program is written for one: setup_inputs(seed, part) draws one part's arguments, and reference() takes and returns one part's arrays. A program takes and returns all parts, laid end to end along the dimension named above; each array names one. Nothing has to cross between parts.
Inputs may be any that keep to these rules, and one draw needn't show every extreme that they name: `counts`: each band block has at least 128 valid frames; some block is full and some has exactly 128. reach[b] never passes the last block of the stream; some block reaches 2 blocks ahead.
All inputs are finite; a program needn't handle non-finite values.
Results may differ from the reference program's by a relative error of at most 0.012.
Values may be sent and summed in bfloat16 or wider, within the bound.
A program may use at most 64 MiB of HBM per device.

```python
import math
import jax
import jax.numpy as jnp
from jax import lax

FEAT = 256
K = 128
BLOCK = 512
MAXREACH = 2
ITERS = 3
BLK_DEV = 4
NBLK = 64
FRAMES = 32768


def draw_features(key, part):
    key = jax.random.fold_in(key, 13)
    key_list = jax.random.split(key, 4)
    frequency = jnp.exp(jax.random.uniform(key_list[0], (4, FEAT), jnp.float32, math.log(0.1), math.log(2.0))) / BLOCK
    phases = jax.random.uniform(key_list[1], (4, FEAT), jnp.float32, -math.pi, math.pi)
    amplitude = jax.random.uniform(key_list[2], (4, FEAT), jnp.float32, 0.5, 1.2)
    position = jnp.arange(FRAMES, dtype=jnp.float32)[:, None]
    smooth_part = jnp.zeros((FRAMES, FEAT), jnp.float32)
    for term_index in range(4):
        smooth_part = smooth_part + amplitude[term_index][None, :] * jnp.cos(position * frequency[term_index][None, :] + phases[term_index][None, :])
    jitter = jnp.clip(jax.random.normal(key_list[3], (FRAMES, FEAT), jnp.float32), -4.0, 4.0) * 0.8
    return (smooth_part + jitter).astype(jnp.bfloat16)


def draw_counts(key, part):
    key = jax.random.fold_in(key, 11)
    values = jax.random.randint(key, (NBLK,), BLOCK // 4, BLOCK + 1)
    values = values.at[0].set(BLOCK)
    values = values.at[1].set(BLOCK // 4)
    return values.astype(jnp.int32)


def draw_reach(key, part):
    key = jax.random.fold_in(key, 12)
    first, second = jax.random.split(key)
    busy = jax.random.randint(first, (NBLK // BLK_DEV,), 0, 2)
    busy = jnp.repeat(busy, BLK_DEV)
    light = jax.random.randint(second, (NBLK,), 0, MAXREACH)
    values = jnp.where(busy == 1, MAXREACH, light)
    values = values.at[0].set(MAXREACH)
    limit = NBLK - 1 - jnp.arange(NBLK, dtype=jnp.int32)
    return jnp.minimum(values, limit).astype(jnp.int32)


def level_of(own_key, shape, pieces, smallest, top_value):
    level = 1.0
    for axis_at, shards_of in pieces:
        steps = jax.random.uniform(jax.random.fold_in(jax.random.fold_in(own_key, 6), axis_at), (shards_of,), jnp.float32, smallest / len(pieces), top_value / len(pieces))
        level = level * jnp.repeat(jnp.exp(steps), shape[axis_at] // shards_of).reshape((-1,) + (1,) * (len(shape) - 1 - axis_at))
    return level


def noise(own_key, dims, deviation, bound, cuts=(), kind=jnp.bfloat16):
    gain = level_of(own_key, dims, cuts, -0.22, 0.18) if cuts else 1.0
    drawn = jax.random.normal(own_key, dims, jnp.float32) * deviation * gain
    return jnp.minimum(jnp.maximum(drawn, -bound), bound).astype(kind)


def setup_inputs(seed: int = 0, part: int = 0) -> dict:
    keys = jax.random.split(jax.random.key(seed), 5)
    part_splits = jax.random.split(jax.random.fold_in(keys[4], part), 5)
    features = draw_features(jax.random.fold_in(jax.random.fold_in(keys[4], part), 71), part)
    start_block = noise(part_splits[1], (FRAMES, K), 1.0, 6.0, ((0, 16),))
    counts = draw_counts(jax.random.fold_in(jax.random.fold_in(keys[4], part), 71), part)
    reach = draw_reach(jax.random.fold_in(jax.random.fold_in(keys[4], part), 71), part)
    return dict(features=features, start_block=start_block, counts=counts, reach=reach)


def affinity(row_x, row_m, col_x, col_m, gamma):
    row_n = lax.optimization_barrier(jnp.sum(jnp.square(row_x.astype(jnp.float32)), 1))
    col_n = lax.optimization_barrier(jnp.sum(jnp.square(col_x.astype(jnp.float32)), 1))
    inner = lax.dot_general(row_x.astype(jnp.float32), col_x.astype(jnp.float32), (((1,), (1,)), ((), ())), preferred_element_type=jnp.float32)
    dist = row_n[:, None] + col_n[None, :] - 2.0 * inner
    return jnp.exp(-gamma * dist) * row_m[:, None] * col_m[None, :]

def reference(features, start_block, counts, reach):
    nblk = counts.shape[0]
    total = features.shape[0]
    gamma = 1.0 / FEAT
    valid = (jnp.arange(BLOCK, dtype=jnp.int32)[None, :] < counts[:, None]).astype(jnp.float32).reshape(total)
    vec = start_block
    basis = jnp.zeros((total, K), jnp.float32)
    proj = jnp.zeros((K, K), jnp.float32)
    for step in range(ITERS):

        def row_step(blk, acc):
            rstart = (blk * BLOCK).astype(jnp.int32)
            row_x = lax.dynamic_slice_in_dim(features, rstart, BLOCK, 0)
            row_m = lax.dynamic_slice_in_dim(valid, rstart, BLOCK, 0)
            row_v = lax.dynamic_slice_in_dim(vec, rstart, BLOCK, 0)
            for off in range(MAXREACH + 1):
                col = jnp.minimum(blk + off, nblk - 1).astype(jnp.int32)
                cstart = (col * BLOCK).astype(jnp.int32)
                col_x = lax.dynamic_slice_in_dim(features, cstart, BLOCK, 0)
                col_m = lax.dynamic_slice_in_dim(valid, cstart, BLOCK, 0)
                col_v = lax.dynamic_slice_in_dim(vec, cstart, BLOCK, 0)
                tile = affinity(row_x, row_m, col_x, col_m, gamma)
                if off > 0:
                    tile = tile * (off <= reach[blk]).astype(jnp.float32)
                tile = tile.astype(jnp.bfloat16)
                fwd = jnp.dot(tile.astype(jnp.float32), col_v.astype(jnp.float32), preferred_element_type=jnp.float32)
                acc = lax.dynamic_update_slice_in_dim(acc, lax.dynamic_slice_in_dim(acc, rstart, BLOCK, 0) + fwd, rstart, 0)
                if off > 0:
                    back = lax.dot_general(tile.astype(jnp.float32), row_v.astype(jnp.float32), (((0,), (0,)), ((), ())), preferred_element_type=jnp.float32)
                    acc = lax.dynamic_update_slice_in_dim(acc, lax.dynamic_slice_in_dim(acc, cstart, BLOCK, 0) + back, cstart, 0)
            return acc
        image = lax.fori_loop(0, nblk, row_step, jnp.zeros((total, K), jnp.float32))
        gram = lax.dot_general(image.astype(jnp.float32), image.astype(jnp.float32), (((0,), (0,)), ((), ())), precision=lax.Precision.HIGHEST, preferred_element_type=jnp.float32)
        proj = lax.dot_general(vec.astype(jnp.float32), image.astype(jnp.float32), (((0,), (0,)), ((), ())), precision=lax.Precision.HIGHEST, preferred_element_type=jnp.float32)
        low = jnp.linalg.cholesky(gram)
        basis = jax.scipy.linalg.solve_triangular(low, image.T, lower=True).T * math.sqrt(total)
        vec = basis.astype(jnp.bfloat16)
    return (basis, proj / (total * BLOCK))
```

```python
import functools
import math

import jax
import jax.numpy as jnp
from jax import lax
from jax.experimental import pallas as pl
from jax.experimental.pallas import tpu as pltpu
from jax.sharding import PartitionSpec as P

BLOCK = 512
MAXREACH = 2
ITERS = 3
OFFS = 2 * MAXREACH + 1
LANE = 128
SUB = 8
ROWS = 128
OFF = -1e30
HI = lax.Precision.HIGHEST
F32 = jnp.float32
BF16 = jnp.bfloat16
NN = (((1,), (0,)), ((), ()))
NT = (((1,), (1,)), ((), ()))
TN = (((0,), (0,)), ((), ()))


def dot(left, right, dims, precision=None):
    return lax.dot_general(left, right, dims, precision=precision, preferred_element_type=F32)


def inverse_factor(gram):
    width = gram.shape[0]
    count = width // SUB
    mat = [gram[SUB * i : SUB * (i + 1), :] for i in range(count)]
    sub = lax.broadcasted_iota(jnp.int32, (SUB, width), 0)
    lane = lax.broadcasted_iota(jnp.int32, (SUB, width), 1)

    def down(value, k):
        return jnp.broadcast_to(value[k : k + 1, :], (SUB, width))

    def across(value, c):
        return jnp.broadcast_to(value[:, c : c + 1], (SUB, width))

    for b in range(count):
        first = SUB * b
        inside = (lane >= first) & (lane < first + SUB)
        cols = [[across(mat[i], first + k) for k in range(SUB)] for i in range(b, count)]
        panel = jnp.where(inside, jnp.where(lane == first + sub, 1.0, 0.0), mat[b])
        for i in range(b + 1, count):
            mat[i] = jnp.where(inside, 0.0, mat[i])
        for k in range(SUB):
            scale = lax.rsqrt(down(cols[0][k], k))
            for col in cols:
                col[k] = col[k] * scale
            for m in range(k + 1, SUB):
                factor = down(cols[0][k], m)
                for col in cols:
                    col[m] = col[m] - col[k] * factor
            row = down(panel, k) * scale
            panel = jnp.where(
                sub == k, row, jnp.where(sub > k, panel - cols[0][k] * row, panel)
            )
            for i in range(b + 1, count):
                mat[i] = mat[i] - cols[i - b][k] * row
        mat[b] = jnp.where(lane < first + SUB, panel, 0.0)
    return jnp.concatenate(mat, 0)


def kernel(
    n, axis, counts, reach, x_hbm, v_hbm, basis_ref, ray_ref,
    xext, vext, meta, oper, image, cbias, rbias, part, parts_in, chunk, whole, pbuf,
    lsem, hsend, hrecv, rsend, rrecv, gsend, grecv, csend, crecv,
):
    nblk = counts.shape[0]
    width = vext.shape[-1]
    feat = xext.shape[-1]
    total = n * nblk * BLOCK
    ext = nblk + 2 * MAXREACH
    size = parts_in.shape[1]
    groups = n // size
    me = lax.axis_index(axis)
    rank = lax.rem(me, size)
    base = me - rank
    has_left = me > 0
    has_right = me < n - 1

    def peer(step):
        return base + lax.rem(rank + step, size)

    def group_peer(step):
        return lax.rem(me + step * size, n)

    own_x = pltpu.make_async_copy(x_hbm, xext.at[pl.ds(MAXREACH, nblk)], lsem.at[0])
    own_v = pltpu.make_async_copy(v_hbm, vext.at[0, pl.ds(MAXREACH, nblk)], lsem.at[1])
    own_x.start()
    own_v.start()

    for j in range(nblk):
        meta[1, j : j + 1, :] = jnp.full((1, LANE), counts[j]).astype(F32)
        meta[1, nblk + j : nblk + j + 1, :] = jnp.full((1, LANE), reach[j]).astype(F32)

    @pl.when(jnp.logical_not(has_left))
    def _():
        meta[0] = jnp.zeros_like(meta[0])
        xext[0:MAXREACH] = jnp.zeros((MAXREACH, BLOCK, feat), BF16)
        for s in range(ITERS):
            vext[s, 0:MAXREACH] = jnp.zeros((MAXREACH, BLOCK, width), BF16)

    @pl.when(jnp.logical_not(has_right))
    def _():
        meta[2] = jnp.zeros_like(meta[2])
        xext[ext - MAXREACH : ext] = jnp.zeros((MAXREACH, BLOCK, feat), BF16)
        for s in range(ITERS):
            vext[s, ext - MAXREACH : ext] = jnp.zeros((MAXREACH, BLOCK, width), BF16)

    barrier = pltpu.get_barrier_semaphore()
    for step in range(1, size):
        pl.semaphore_signal(barrier, inc=1, device_id={axis: peer(step)}, device_id_type=pl.DeviceIdType.MESH)
    for step in range(1, groups):
        pl.semaphore_signal(barrier, inc=1, device_id={axis: group_peer(step)}, device_id_type=pl.DeviceIdType.MESH)

    @pl.when(has_left)
    def _():
        pl.semaphore_signal(barrier, inc=1, device_id={axis: me - 1}, device_id_type=pl.DeviceIdType.MESH)

    @pl.when(has_right)
    def _():
        pl.semaphore_signal(barrier, inc=1, device_id={axis: me + 1}, device_id_type=pl.DeviceIdType.MESH)

    pl.semaphore_wait(
        barrier, size - 1 + groups - 1 + has_left.astype(jnp.int32) + has_right.astype(jnp.int32)
    )

    def copy(src, dst, sem_row, sem_col, target):
        return pltpu.make_async_remote_copy(
            src_ref=src, dst_ref=dst, send_sem=hsend.at[sem_row, sem_col],
            recv_sem=hrecv.at[sem_row, sem_col], device_id={axis: target},
            device_id_type=pl.DeviceIdType.MESH,
        )

    def halo(row, source, dest, j, left):
        if left:
            return copy(source(j), dest(ext - MAXREACH + j), row, MAXREACH + j, me - 1)
        return copy(source(nblk - MAXREACH + j), dest(j), row, j, me + 1)

    def x_halo(j, left):
        return halo(ITERS, lambda b: x_hbm.at[b], lambda b: xext.at[b], j, left)

    def v_halo(s, j, left):
        if s == 0:
            return halo(s, lambda b: v_hbm.at[b], lambda b: vext.at[s, b], j, left)
        return halo(s, lambda b: vext.at[s, MAXREACH + b], lambda b: vext.at[s, b], j, left)

    def m_halo(left):
        if left:
            return copy(meta.at[1], meta.at[2], ITERS + 1, 1, me - 1)
        return copy(meta.at[1], meta.at[0], ITERS + 1, 0, me + 1)

    near = [(j, True) for j in range(MAXREACH)], [(j, False) for j in reversed(range(MAXREACH))]

    def each(left, action):
        @pl.when(has_left if left else has_right)
        def _():
            action()

    def comes(left, action):
        @pl.when(has_right if left else has_left)
        def _():
            action()

    for left in (True, False):
        def start(left=left):
            m_halo(left).start()
            for j, side in near[0 if left else 1]:
                x_halo(j, side).start()
            for j, side in near[0 if left else 1]:
                v_halo(0, j, side).start()
        each(left, start)

    gamma2 = math.log2(math.e) / feat

    def col_bias(e):
        xe = xext[e].astype(F32)
        norm = dot(jnp.ones((SUB, feat), F32), xe * xe, NT, HI)
        side, j = (0, nblk - MAXREACH + e) if e < MAXREACH else (
            (1, e - MAXREACH) if e < nblk + MAXREACH else (2, e - nblk - MAXREACH))
        held = jnp.concatenate([meta[side, j : j + 1, :]] * (BLOCK // LANE), 1)
        at = lax.broadcasted_iota(jnp.int32, (1, BLOCK), 1).astype(F32)
        cbias[e : e + 1, :] = jnp.where(at < held, -gamma2 * norm[0:1, :], OFF)

    def row_bias(i):
        xe = xext[MAXREACH + i].astype(F32)
        norm = jnp.sum(xe * xe, 1, keepdims=True)
        at = lax.broadcasted_iota(jnp.int32, (BLOCK, 1), 0).astype(F32)
        rbias[i] = jnp.where(at < meta[1, i : i + 1, 0:1], -gamma2 * norm, OFF)

    def tiles(i, offsets):
        bias = []
        for o in offsets:
            d = o - MAXREACH
            if d >= 0:
                far = meta[1, nblk + i : nblk + i + 1, :]
            else:
                b = i + d
                far = meta[1, nblk + b : nblk + b + 1, :] if b >= 0 else meta[0, 2 * nblk + b : 2 * nblk + b + 1, :]
            far = jnp.concatenate([far] * (BLOCK // LANE), 1)
            bias.append(jnp.where(far >= float(abs(d)), cbias[i + o : i + o + 1, :], OFF))

        def rows_step(r, carry):
            at = pl.multiple_of(r * ROWS, ROWS)
            rows = xext[MAXREACH + i, pl.ds(at, ROWS), :]
            left = rbias[i, pl.ds(at, ROWS), :]
            for o, right in zip(offsets, bias):
                inner = dot(rows, xext[i + o], NT)
                oper[i, pl.ds(at, ROWS), o * BLOCK : (o + 1) * BLOCK] = jnp.exp2(
                    inner * (2.0 * gamma2) + (left + right)
                ).astype(BF16)
            return carry

        lax.fori_loop(0, BLOCK // ROWS, rows_step, 0)

    own = [[o for o in range(OFFS) if MAXREACH <= i + o < nblk + MAXREACH] for i in range(nblk)]
    edge = [[o for o in range(OFFS) if o not in own[i]] for i in range(nblk)]

    own_x.wait()
    for j in range(nblk):
        col_bias(MAXREACH + j)
        row_bias(j)
    for i in range(nblk):
        tiles(i, own[i])
    for left in (True, False):
        def arrive(left=left):
            m_halo(left).wait_recv()
            for j, side in near[0 if left else 1]:
                x_halo(j, side).wait_recv()
        comes(left, arrive)
    for e in list(range(MAXREACH)) + list(range(ext - MAXREACH, ext)):
        col_bias(e)
    for i in range(nblk):
        tiles(i, edge[i])
    own_v.wait()

    def product(s, i, offsets):
        first, last = offsets[0], offsets[-1] + 1
        vec = vext[s, i + first : i + last].reshape((last - first) * BLOCK, width)
        return dot(oper[i, :, first * BLOCK : last * BLOCK], vec, NN)

    def reduce_start(s, which):
        for step in range(1, size):
            q = lax.rem(rank + step, size)
            pltpu.make_async_remote_copy(
                src_ref=part.at[s, which, q], dst_ref=parts_in.at[2 * s + which, rank],
                send_sem=rsend.at[2 * s + which, step], recv_sem=rrecv.at[2 * s + which, rank],
                device_id={axis: base + q}, device_id_type=pl.DeviceIdType.MESH,
            ).start()

    def reduce_rest(s, which):
        row = 2 * s + which

        def incoming(q):
            return pltpu.make_async_remote_copy(
                src_ref=part.at[s, which, q], dst_ref=parts_in.at[row, q],
                send_sem=rsend.at[row, 0], recv_sem=rrecv.at[row, q],
                device_id={axis: base + q}, device_id_type=pl.DeviceIdType.MESH,
            )

        total_chunk = part[s, which, rank]
        for step in range(1, size):
            q = lax.rem(rank + step, size)
            incoming(q).wait_recv()
            total_chunk = total_chunk + parts_in[row, q]
        if groups > 1:
            me_group = me // size
            chunk[row, me_group] = total_chunk

            def cross(step):
                return pltpu.make_async_remote_copy(
                    src_ref=chunk.at[row, me_group], dst_ref=chunk.at[row, me_group],
                    send_sem=csend.at[row, step], recv_sem=crecv.at[row, step],
                    device_id={axis: group_peer(step)}, device_id_type=pl.DeviceIdType.MESH,
                )

            for step in range(1, groups):
                cross(step).start()
            for step in range(1, groups):
                cross(step).wait_recv()
            total_chunk = chunk[row, 0]
            for g in range(1, groups):
                total_chunk = total_chunk + chunk[row, g]
            for step in range(1, groups):
                cross(step).wait_send()
        whole[row, rank] = total_chunk

        def gather(step, q):
            return pltpu.make_async_remote_copy(
                src_ref=whole.at[row, rank], dst_ref=whole.at[row, rank],
                send_sem=gsend.at[row, step], recv_sem=grecv.at[row, rank],
                device_id={axis: base + q}, device_id_type=pl.DeviceIdType.MESH,
            )

        for step in range(1, size):
            gather(step, lax.rem(rank + step, size)).start()

    def reduce_done(s, which):
        row = 2 * s + which
        for step in range(1, size):
            q = lax.rem(rank + step, size)
            pltpu.make_async_remote_copy(
                src_ref=whole.at[row, q], dst_ref=whole.at[row, q],
                send_sem=gsend.at[row, step], recv_sem=grecv.at[row, q],
                device_id={axis: base + q}, device_id_type=pl.DeviceIdType.MESH,
            ).wait_recv()
        return jnp.concatenate([whole[row, q] for q in range(size)], 0)

    def reduce_clear(s, which):
        row = 2 * s + which
        for step in range(1, size):
            q = lax.rem(rank + step, size)
            pltpu.make_async_remote_copy(
                src_ref=part.at[s, which, q], dst_ref=parts_in.at[row, rank],
                send_sem=rsend.at[row, step], recv_sem=rrecv.at[row, rank],
                device_id={axis: base + q}, device_id_type=pl.DeviceIdType.MESH,
            ).wait_send()
            pltpu.make_async_remote_copy(
                src_ref=whole.at[row, rank], dst_ref=whole.at[row, rank],
                send_sem=gsend.at[row, step], recv_sem=grecv.at[row, rank],
                device_id={axis: base + q}, device_id_type=pl.DeviceIdType.MESH,
            ).wait_send()

    def split(value):
        return value.reshape(size, width // size, width)

    order = [j for pair in zip(range(nblk), reversed(range(nblk))) for j in pair][:nblk]
    for s in range(ITERS):
        for i in range(nblk):
            image[i] = product(s, i, own[i])
        for left in (True, False):
            def arrive(left=left, s=s):
                for j, side in near[0 if left else 1]:
                    v_halo(s, j, side).wait_recv()
            comes(left, arrive)
        gram = None
        for i in range(nblk):
            if edge[i]:
                runs = [[o for o in edge[i] if i + o < MAXREACH], [o for o in edge[i] if i + o >= MAXREACH]]
                value = image[i]
                for run in runs:
                    if run:
                        value = value + product(s, i, run)
                image[i] = value
            else:
                value = image[i]
            term = dot(value, value, TN, HI)
            gram = term if gram is None else gram + term
        part[s, 0] = split(gram)
        reduce_start(s, 0)
        if s == ITERS - 1:
            proj = None
            for i in range(nblk):
                term = dot(vext[s, MAXREACH + i].astype(F32), image[i], TN, HI)
                proj = term if proj is None else proj + term
            part[s, 1] = split(proj)
            reduce_start(s, 1)
        reduce_rest(s, 0)
        if s == ITERS - 1:
            reduce_rest(s, 1)
        gram = reduce_done(s, 0)
        inv = inverse_factor(gram) * math.sqrt(total)
        for i in order:
            basis = dot(image[i], inv, NT, HI)
            if s == ITERS - 1:
                basis_ref[i] = basis
                continue
            vext[s + 1, MAXREACH + i] = basis.astype(BF16)
            if i < MAXREACH:
                each(True, lambda s=s, i=i: v_halo(s + 1, i, True).start())
            if i >= nblk - MAXREACH:
                each(False, lambda s=s, i=i: v_halo(s + 1, i - nblk + MAXREACH, False).start())
    ray_ref[...] = reduce_done(ITERS - 1, 1) * (1.0 / (total * BLOCK))

    for s in range(ITERS):
        reduce_clear(s, 0)
    reduce_clear(ITERS - 1, 1)
    for left in (True, False):
        def finish(left=left):
            m_halo(left).wait_send()
            for j, side in near[0 if left else 1]:
                x_halo(j, side).wait_send()
                for s in range(ITERS):
                    v_halo(s, j, side).wait_send()
        each(left, finish)


def local(axis, features, start_block, counts, reach):
    n = lax.axis_size(axis)
    nblk = counts.shape[0]
    rows, feat = features.shape
    width = start_block.shape[1]
    ext = nblk + 2 * MAXREACH
    size = min(n, width // SUB)
    groups = n // size
    rung = width // size
    sems = pltpu.SemaphoreType.DMA
    any_spec = pl.BlockSpec(memory_space=pl.ANY)
    smem = pl.BlockSpec(memory_space=pltpu.SMEM)
    vmem = pl.BlockSpec(memory_space=pltpu.VMEM)
    rounds = 2 * ITERS
    basis, ray = pl.pallas_call(
        functools.partial(kernel, n, axis),
        out_shape=(
            jax.ShapeDtypeStruct((nblk, BLOCK, width), F32),
            jax.ShapeDtypeStruct((width, width), F32),
        ),
        in_specs=[smem, smem, any_spec, any_spec],
        out_specs=(vmem, vmem),
        scratch_shapes=[
            pltpu.VMEM((ext, BLOCK, feat), BF16),
            pltpu.VMEM((ITERS, ext, BLOCK, width), BF16),
            pltpu.VMEM((3, 2 * nblk, LANE), F32),
            pltpu.VMEM((nblk, BLOCK, OFFS * BLOCK), BF16),
            pltpu.VMEM((nblk, BLOCK, width), F32),
            pltpu.VMEM((ext, BLOCK), F32),
            pltpu.VMEM((nblk, BLOCK, 1), F32),
            pltpu.VMEM((ITERS, 2, size, rung, width), F32),
            pltpu.VMEM((rounds, size, rung, width), F32),
            pltpu.VMEM((rounds, groups, rung, width), F32),
            pltpu.VMEM((rounds, size, rung, width), F32),
            pltpu.VMEM((SUB, LANE), F32),
            sems((2,)),
            sems((ITERS + 2, 2 * MAXREACH)),
            sems((ITERS + 2, 2 * MAXREACH)),
            sems((rounds, size)),
            sems((rounds, size)),
            sems((rounds, size)),
            sems((rounds, size)),
            sems((rounds, groups)),
            sems((rounds, groups)),
        ],
        compiler_params=pltpu.CompilerParams(
            collective_id=0, has_side_effects=True, vmem_limit_bytes=48 * 1024 * 1024
        ),
    )(counts, reach, features.reshape(nblk, BLOCK, feat), start_block.reshape(nblk, BLOCK, width))
    return basis.reshape(rows, width), ray


def solution(mesh):
    in_specs = (
        P(("streams", "frames"), None),
        P(("streams", "frames"), None),
        P(("streams", "frames")),
        P(("streams", "frames")),
    )
    out_specs = (P(("streams", "frames"), None), P("streams", None))
    return jax.shard_map(
        functools.partial(local, "frames"), mesh=mesh, in_specs=in_specs, out_specs=out_specs, check_vma=False
    )
```

```python
import functools
import math

import jax
import jax.numpy as jnp
from jax import lax
from jax.experimental import pallas as pl
from jax.experimental.pallas import tpu as pltpu
from jax.sharding import PartitionSpec as P

BLOCK = 512
MAXREACH = 2
ITERS = 3
OFFS = 2 * MAXREACH + 1
LANE = 128
SUB = 8
ROWS = 128
OFF = -1e30
HI = lax.Precision.HIGHEST
F32 = jnp.float32
BF16 = jnp.bfloat16
NN = (((1,), (0,)), ((), ()))
NT = (((1,), (1,)), ((), ()))
TN = (((0,), (0,)), ((), ()))


def dot(left, right, dims, precision=None):
    return lax.dot_general(left, right, dims, precision=precision, preferred_element_type=F32)


def inverse_factor(gram):
    width = gram.shape[0]
    count = width // SUB
    mat = [gram[SUB * i : SUB * (i + 1), :] for i in range(count)]
    sub = lax.broadcasted_iota(jnp.int32, (SUB, width), 0)
    lane = lax.broadcasted_iota(jnp.int32, (SUB, width), 1)

    def down(value, k):
        return jnp.broadcast_to(value[k : k + 1, :], (SUB, width))

    def across(value, c):
        return jnp.broadcast_to(value[:, c : c + 1], (SUB, width))

    for b in range(count):
        first = SUB * b
        inside = (lane >= first) & (lane < first + SUB)
        cols = [[across(mat[i], first + k) for k in range(SUB)] for i in range(b, count)]
        panel = jnp.where(inside, jnp.where(lane == first + sub, 1.0, 0.0), mat[b])
        for i in range(b + 1, count):
            mat[i] = jnp.where(inside, 0.0, mat[i])
        for k in range(SUB):
            scale = lax.rsqrt(down(cols[0][k], k))
            for col in cols:
                col[k] = col[k] * scale
            for m in range(k + 1, SUB):
                factor = down(cols[0][k], m)
                for col in cols:
                    col[m] = col[m] - col[k] * factor
            row = down(panel, k) * scale
            panel = jnp.where(
                sub == k, row, jnp.where(sub > k, panel - cols[0][k] * row, panel)
            )
            for i in range(b + 1, count):
                mat[i] = mat[i] - cols[i - b][k] * row
        mat[b] = jnp.where(lane < first + SUB, panel, 0.0)
    return jnp.concatenate(mat, 0)


def kernel(
    n, axis, counts, reach, x_hbm, v_hbm, basis_ref, ray_ref,
    xext, vext, meta, oper, image, cbias, rbias, part, parts_in, chunk, whole, pbuf,
    lsem, hsend, hrecv, rsend, rrecv, gsend, grecv, csend, crecv,
):
    nblk = counts.shape[0]
    width = vext.shape[-1]
    feat = xext.shape[-1]
    total = n * nblk * BLOCK
    ext = nblk + 2 * MAXREACH
    size = parts_in.shape[1]
    groups = n // size
    me = lax.axis_index(axis)
    rank = lax.rem(me, size)
    base = me - rank
    has_left = me > 0
    has_right = me < n - 1

    def peer(step):
        return base + lax.rem(rank + step, size)

    def group_peer(step):
        return lax.rem(me + step * size, n)

    own_x = pltpu.make_async_copy(x_hbm, xext.at[pl.ds(MAXREACH, nblk)], lsem.at[0])
    own_v = pltpu.make_async_copy(v_hbm, vext.at[0, pl.ds(MAXREACH, nblk)], lsem.at[1])
    own_x.start()
    own_v.start()

    for j in range(nblk):
        meta[1, j : j + 1, :] = jnp.full((1, LANE), counts[j]).astype(F32)
        meta[1, nblk + j : nblk + j + 1, :] = jnp.full((1, LANE), reach[j]).astype(F32)

    @pl.when(jnp.logical_not(has_left))
    def _():
        meta[0] = jnp.zeros_like(meta[0])
        xext[0:MAXREACH] = jnp.zeros((MAXREACH, BLOCK, feat), BF16)
        for s in range(ITERS - 1):
            image[s, 0:MAXREACH] = jnp.zeros((MAXREACH, BLOCK, width), F32)
        vext[0, 0:MAXREACH] = jnp.zeros((MAXREACH, BLOCK, width), BF16)

    @pl.when(jnp.logical_not(has_right))
    def _():
        meta[2] = jnp.zeros_like(meta[2])
        xext[ext - MAXREACH : ext] = jnp.zeros((MAXREACH, BLOCK, feat), BF16)
        for s in range(ITERS - 1):
            image[s, ext - MAXREACH : ext] = jnp.zeros((MAXREACH, BLOCK, width), F32)
        vext[0, ext - MAXREACH : ext] = jnp.zeros((MAXREACH, BLOCK, width), BF16)

    barrier = pltpu.get_barrier_semaphore()
    for step in range(1, size):
        pl.semaphore_signal(barrier, inc=1, device_id={axis: peer(step)}, device_id_type=pl.DeviceIdType.MESH)
    for step in range(1, groups):
        pl.semaphore_signal(barrier, inc=1, device_id={axis: group_peer(step)}, device_id_type=pl.DeviceIdType.MESH)

    @pl.when(has_left)
    def _():
        pl.semaphore_signal(barrier, inc=1, device_id={axis: me - 1}, device_id_type=pl.DeviceIdType.MESH)

    @pl.when(has_right)
    def _():
        pl.semaphore_signal(barrier, inc=1, device_id={axis: me + 1}, device_id_type=pl.DeviceIdType.MESH)

    pl.semaphore_wait(
        barrier, size - 1 + groups - 1 + has_left.astype(jnp.int32) + has_right.astype(jnp.int32)
    )

    def copy(src, dst, sem_row, sem_col, target):
        return pltpu.make_async_remote_copy(
            src_ref=src, dst_ref=dst, send_sem=hsend.at[sem_row, sem_col],
            recv_sem=hrecv.at[sem_row, sem_col], device_id={axis: target},
            device_id_type=pl.DeviceIdType.MESH,
        )

    def halo(row, source, dest, j, left):
        if left:
            return copy(source(j), dest(ext - MAXREACH + j), row, MAXREACH + j, me - 1)
        return copy(source(nblk - MAXREACH + j), dest(j), row, j, me + 1)

    def x_halo(j, left):
        return halo(ITERS, lambda b: x_hbm.at[b], lambda b: xext.at[b], j, left)

    def v_halo(j, left):
        return halo(ITERS - 1, lambda b: v_hbm.at[b], lambda b: vext.at[0, b], j, left)

    def i_halo(s, j, left):
        return halo(s, lambda b: image.at[s, MAXREACH + b], lambda b: image.at[s, b], j, left)

    def m_halo(left):
        if left:
            return copy(meta.at[1], meta.at[2], ITERS + 1, 1, me - 1)
        return copy(meta.at[1], meta.at[0], ITERS + 1, 0, me + 1)

    near = [(j, True) for j in range(MAXREACH)], [(j, False) for j in reversed(range(MAXREACH))]

    def each(left, action):
        @pl.when(has_left if left else has_right)
        def _():
            action()

    def comes(left, action):
        @pl.when(has_right if left else has_left)
        def _():
            action()

    for left in (True, False):
        def start(left=left):
            m_halo(left).start()
            for j, side in near[0 if left else 1]:
                x_halo(j, side).start()
            for j, side in near[0 if left else 1]:
                v_halo(j, side).start()
        each(left, start)

    gamma2 = math.log2(math.e) / feat

    def col_bias(e):
        xe = xext[e].astype(F32)
        norm = dot(jnp.ones((SUB, feat), F32), xe * xe, NT, HI)
        side, j = (0, nblk - MAXREACH + e) if e < MAXREACH else (
            (1, e - MAXREACH) if e < nblk + MAXREACH else (2, e - nblk - MAXREACH))
        held = jnp.concatenate([meta[side, j : j + 1, :]] * (BLOCK // LANE), 1)
        at = lax.broadcasted_iota(jnp.int32, (1, BLOCK), 1).astype(F32)
        cbias[e : e + 1, :] = jnp.where(at < held, -gamma2 * norm[0:1, :], OFF)

    def row_bias(i):
        xe = xext[MAXREACH + i].astype(F32)
        norm = jnp.sum(xe * xe, 1, keepdims=True)
        at = lax.broadcasted_iota(jnp.int32, (BLOCK, 1), 0).astype(F32)
        rbias[i] = jnp.where(at < meta[1, i : i + 1, 0:1], -gamma2 * norm, OFF)

    def tiles(i, offsets):
        bias = []
        for o in offsets:
            d = o - MAXREACH
            if d >= 0:
                far = meta[1, nblk + i : nblk + i + 1, :]
            else:
                b = i + d
                far = meta[1, nblk + b : nblk + b + 1, :] if b >= 0 else meta[0, 2 * nblk + b : 2 * nblk + b + 1, :]
            far = jnp.concatenate([far] * (BLOCK // LANE), 1)
            bias.append(jnp.where(far >= float(abs(d)), cbias[i + o : i + o + 1, :], OFF))

        def rows_step(r, carry):
            at = pl.multiple_of(r * ROWS, ROWS)
            rows = xext[MAXREACH + i, pl.ds(at, ROWS), :]
            left = rbias[i, pl.ds(at, ROWS), :]
            for o, right in zip(offsets, bias):
                inner = dot(rows, xext[i + o], NT)
                oper[i, pl.ds(at, ROWS), o * BLOCK : (o + 1) * BLOCK] = jnp.exp2(
                    inner * (2.0 * gamma2) + (left + right)
                ).astype(BF16)
            return carry

        lax.fori_loop(0, BLOCK // ROWS, rows_step, 0)

    own = [[o for o in range(OFFS) if MAXREACH <= i + o < nblk + MAXREACH] for i in range(nblk)]
    edge = [[o for o in range(OFFS) if o not in own[i]] for i in range(nblk)]

    own_x.wait()
    for j in range(nblk):
        col_bias(MAXREACH + j)
        row_bias(j)
    for i in range(nblk):
        tiles(i, own[i])
    for left in (True, False):
        def arrive(left=left):
            m_halo(left).wait_recv()
            for j, side in near[0 if left else 1]:
                x_halo(j, side).wait_recv()
        comes(left, arrive)
    for e in list(range(MAXREACH)) + list(range(ext - MAXREACH, ext)):
        col_bias(e)
    for i in range(nblk):
        tiles(i, edge[i])
    own_v.wait()

    def product(s, i, offsets):
        first, last = offsets[0], offsets[-1] + 1
        vec = vext[s, i + first : i + last].reshape((last - first) * BLOCK, width)
        return dot(oper[i, :, first * BLOCK : last * BLOCK], vec, NN)

    def remote(src, dst, send, recv, q):
        return pltpu.make_async_remote_copy(
            src_ref=src, dst_ref=dst, send_sem=send, recv_sem=recv,
            device_id={axis: base + q}, device_id_type=pl.DeviceIdType.MESH,
        )

    def reduce_start(s, which):
        row = 2 * s + which
        for step in range(1, size):
            q = lax.rem(rank + step, size)
            remote(part.at[s, which, q], parts_in.at[row, step - 1], rsend.at[row], rrecv.at[row], q).start()

    def reduce_rest(s, which):
        row = 2 * s + which
        slots = parts_in.at[row, pl.ds(0, size - 1)]
        remote(slots, slots, rsend.at[row], rrecv.at[row], rank).wait_recv()
        total_chunk = part[s, which, rank]
        for step in range(1, size):
            total_chunk = total_chunk + parts_in[row, step - 1]
        if groups > 1:
            me_group = me // size
            chunk[row, me_group] = total_chunk

            def cross(step):
                return pltpu.make_async_remote_copy(
                    src_ref=chunk.at[row, me_group], dst_ref=chunk.at[row, me_group],
                    send_sem=csend.at[row, step], recv_sem=crecv.at[row, step],
                    device_id={axis: group_peer(step)}, device_id_type=pl.DeviceIdType.MESH,
                )

            for step in range(1, groups):
                cross(step).start()
            for step in range(1, groups):
                cross(step).wait_recv()
            total_chunk = chunk[row, 0]
            for g in range(1, groups):
                total_chunk = total_chunk + chunk[row, g]
            for step in range(1, groups):
                cross(step).wait_send()
        whole[row, rank] = total_chunk
        for step in range(1, size):
            q = lax.rem(rank + step, size)
            remote(whole.at[row, rank], whole.at[row, rank], gsend.at[row], grecv.at[row], q).start()

    def reduce_done(s, which):
        row = 2 * s + which
        slots = parts_in.at[row, pl.ds(0, size - 1)]
        remote(slots, slots, gsend.at[row], grecv.at[row], rank).wait_recv()
        return jnp.concatenate([whole[row, q] for q in range(size)], 0)

    def reduce_clear(s, which):
        row = 2 * s + which
        slots = parts_in.at[row, pl.ds(0, size - 1)]
        remote(slots, slots, rsend.at[row], rrecv.at[row], rank).wait_send()
        remote(slots, slots, gsend.at[row], grecv.at[row], rank).wait_send()

    def split(value):
        return value.reshape(size, width // size, width)

    order = [j for pair in zip(range(nblk), reversed(range(nblk))) for j in pair][:nblk]
    inner = list(range(MAXREACH, nblk + MAXREACH))
    for s in range(ITERS):
        for i in range(nblk):
            image[s, MAXREACH + i] = product(s, i, own[i])
        if s == 0:
            for left in (True, False):
                def arrive(left=left):
                    for j, side in near[0 if left else 1]:
                        v_halo(j, side).wait_recv()
                comes(left, arrive)
        for i in order:
            runs = [[o for o in edge[i] if i + o < MAXREACH], [o for o in edge[i] if i + o >= MAXREACH]]
            value = image[s, MAXREACH + i]
            for run in runs:
                if run:
                    value = value + product(s, i, run)
            if edge[i]:
                image[s, MAXREACH + i] = value
        gram = None
        for i in range(nblk):
            value = image[s, MAXREACH + i]
            term = dot(value, value, TN, HI)
            gram = term if gram is None else gram + term
        part[s, 0] = split(gram)
        reduce_start(s, 0)
        if s == ITERS - 1:
            proj = None
            for i in range(nblk):
                term = dot(vext[s, MAXREACH + i].astype(F32), image[s, MAXREACH + i], TN, HI)
                proj = term if proj is None else proj + term
            part[s, 1] = split(proj)
            reduce_start(s, 1)
        reduce_rest(s, 0)
        if s == ITERS - 1:
            reduce_rest(s, 1)
        if s < ITERS - 1:
            for left in (True, False):
                def send(left=left, s=s):
                    for j, side in near[0 if left else 1]:
                        i_halo(s, j, side).start()
                each(left, send)
        gram = reduce_done(s, 0)
        inv = inverse_factor(gram) * math.sqrt(total)
        for e in inner:
            basis = dot(image[s, e], inv, NT, HI)
            if s == ITERS - 1:
                basis_ref[e - MAXREACH] = basis
            else:
                vext[s + 1, e] = basis.astype(BF16)
        if s < ITERS - 1:
            for left in (True, False):
                def arrive(left=left, s=s):
                    for j, side in near[0 if left else 1]:
                        i_halo(s, j, side).wait_recv()
                comes(left, arrive)
            for e in range(ext):
                if e not in inner:
                    vext[s + 1, e] = dot(image[s, e], inv, NT, HI).astype(BF16)
    ray_ref[...] = reduce_done(ITERS - 1, 1) * (1.0 / (total * BLOCK))

    for s in range(ITERS):
        reduce_clear(s, 0)
    reduce_clear(ITERS - 1, 1)
    for left in (True, False):
        def finish(left=left):
            m_halo(left).wait_send()
            for j, side in near[0 if left else 1]:
                x_halo(j, side).wait_send()
                v_halo(j, side).wait_send()
                for s in range(ITERS - 1):
                    i_halo(s, j, side).wait_send()
        each(left, finish)


def local(axis, features, start_block, counts, reach):
    n = lax.axis_size(axis)
    nblk = counts.shape[0]
    rows, feat = features.shape
    width = start_block.shape[1]
    ext = nblk + 2 * MAXREACH
    size = min(n, width // SUB)
    groups = n // size
    rung = width // size
    sems = pltpu.SemaphoreType.DMA
    any_spec = pl.BlockSpec(memory_space=pl.ANY)
    smem = pl.BlockSpec(memory_space=pltpu.SMEM)
    vmem = pl.BlockSpec(memory_space=pltpu.VMEM)
    rounds = 2 * ITERS
    basis, ray = pl.pallas_call(
        functools.partial(kernel, n, axis),
        out_shape=(
            jax.ShapeDtypeStruct((nblk, BLOCK, width), F32),
            jax.ShapeDtypeStruct((width, width), F32),
        ),
        in_specs=[smem, smem, any_spec, any_spec],
        out_specs=(vmem, vmem),
        scratch_shapes=[
            pltpu.VMEM((ext, BLOCK, feat), BF16),
            pltpu.VMEM((ITERS, ext, BLOCK, width), BF16),
            pltpu.VMEM((3, 2 * nblk, LANE), F32),
            pltpu.VMEM((nblk, BLOCK, OFFS * BLOCK), BF16),
            pltpu.VMEM((ITERS, ext, BLOCK, width), F32),
            pltpu.VMEM((ext, BLOCK), F32),
            pltpu.VMEM((nblk, BLOCK, 1), F32),
            pltpu.VMEM((ITERS, 2, size, rung, width), F32),
            pltpu.VMEM((rounds, size, rung, width), F32),
            pltpu.VMEM((rounds, groups, rung, width), F32),
            pltpu.VMEM((rounds, size, rung, width), F32),
            pltpu.VMEM((SUB, LANE), F32),
            sems((2,)),
            sems((ITERS + 2, 2 * MAXREACH)),
            sems((ITERS + 2, 2 * MAXREACH)),
            sems((rounds,)),
            sems((rounds,)),
            sems((rounds,)),
            sems((rounds,)),
            sems((rounds, groups)),
            sems((rounds, groups)),
        ],
        compiler_params=pltpu.CompilerParams(
            collective_id=0, has_side_effects=True, vmem_limit_bytes=60 * 1024 * 1024
        ),
    )(counts, reach, features.reshape(nblk, BLOCK, feat), start_block.reshape(nblk, BLOCK, width))
    return basis.reshape(rows, width), ray


def solution(mesh):
    in_specs = (
        P(("streams", "frames"), None),
        P(("streams", "frames"), None),
        P(("streams", "frames")),
        P(("streams", "frames")),
    )
    out_specs = (P(("streams", "frames"), None), P("streams", None))
    return jax.shard_map(
        functools.partial(local, "frames"), mesh=mesh, in_specs=in_specs, out_specs=out_specs, check_vma=False
    )
```
